32 devices in a mesh: dp: 2 (over core), seq: 16 (over z, y, x).
Axes of the slice: x: 2, y: 2, z: 4, core: 2. Of those that a mesh axis runs over, the one named last changes fastest.
Arguments:
- query: bfloat16 [4096, 4096], P('dp', 'seq'), parts along dimension 0, may hold values from -6 to 6
- key_seq: bfloat16 [4096, 512], P(('dp', 'seq')), parts along dimension 0, may hold values from -6 to 6
- value_seq: bfloat16 [4096, 512], P(('dp', 'seq')), parts along dimension 0, may hold values from -6 to 6
- attn_out: bfloat16 [4096, 4096], P(('dp', 'seq')), parts along dimension 0, may hold values from -6 to 6
- grad_out: bfloat16 [4096, 4096], P(('dp', 'seq')), parts along dimension 0, may hold values from -6 to 6
- lse: float32 [32, 4096], P('seq', 'dp'), parts along dimension 1, as said below
Outputs:
- query_grad: bfloat16 [4096, 4096], P(('dp', 'seq')), parts along dimension 0
- key_grad: bfloat16 [4096, 512], P(('dp', 'seq')), parts along dimension 0
- value_grad: bfloat16 [4096, 512], P(('dp', 'seq')), parts along dimension 0
The draws below stay inside these ranges and needn't reach their ends.
There are 2 independent parts, one for each index of `dp`. The reference program is written for one: setup_inputs(seed, part) draws one part's arguments, and reference() takes and returns one part's arrays. A program takes and returns all parts, laid end to end along the dimension named above; each array names one. Nothing has to cross between parts.
Inputs may be any that keep to these rules, and one draw needn't show every extreme that they name: lse[h, i] is the log of the sum over k <= i of exp(q_h[i] . k_g(h)[k] / sqrt(128)), computed from these query and key_seq arrays.
All inputs are finite; a program needn't handle non-finite values.
Results may differ from the reference program's by a relative error of at most 0.0054.
Values may be sent and summed in bfloat16 or wider, within the bound.
No kernel may reach another device: no remote copies, remote signals or barrier semaphores. Data moves between devices by JAX's collectives and lax.ppermute only.
A program may use at most 128 MiB of HBM per device.

```python
import jax
import jax.numpy as jnp
from jax import lax

H = 32
KVH = 4
DH = 128
TOKENS = 2048


def draw_pair(key):
    query_key = jax.random.fold_in(key, 101)
    keys_key = jax.random.fold_in(key, 102)
    queries = jnp.clip(jax.random.normal(query_key, (TOKENS, H * DH), jnp.float32), -6.0, 6.0)
    keys = jnp.clip(jax.random.normal(keys_key, (TOKENS, KVH * DH), jnp.float32), -6.0, 6.0)
    return (queries.astype(jnp.bfloat16), keys.astype(jnp.bfloat16))


def draw_query(key, part):
    queries, keys = draw_pair(key)
    return queries


def draw_key_seq(key, part):
    queries, keys = draw_pair(key)
    return keys


def draw_lse(key, part):
    queries, keys = draw_pair(key)
    query_heads = queries.astype(jnp.float32).reshape(TOKENS, H, DH)
    key_heads = keys.astype(jnp.float32).reshape(TOKENS, KVH, DH)
    row_ids = jnp.arange(TOKENS, dtype=jnp.int32)
    causal = row_ids[:, None] >= row_ids[None, :]
    group_size = H // KVH

    def one_head(head):
        scores = jnp.dot(query_heads[:, head, :], key_heads[:, head // group_size, :].T, precision=lax.Precision.HIGHEST) * DH ** (-0.5)
        scores = jnp.where(causal, scores, -1e+30)
        return jax.nn.logsumexp(scores, axis=1)
    return lax.map(one_head, jnp.arange(H, dtype=jnp.int32)).astype(jnp.float32)


def level_of(stream_key, dims, cuts, least, largest):
    def one(position, shards_of):
        draws = jax.random.uniform(jax.random.fold_in(jax.random.fold_in(stream_key, 6), position), (shards_of,), jnp.float32, least / len(cuts), largest / len(cuts))
        return jnp.repeat(jnp.exp(draws), dims[position] // shards_of).reshape((-1,) + (1,) * (len(dims) - position - 1))

    gain = one(*cuts[0])
    for cut in cuts[1:]:
        gain = gain * one(*cut)
    return gain


def scatter_about(rng, dims, deviation, limit, cuts=(), kind=jnp.bfloat16):
    loudness = level_of(rng, dims, cuts, -0.22, 0.18) if cuts else 1.0
    drawn = jax.random.normal(rng, dims, jnp.float32) * deviation * loudness
    return jnp.minimum(jnp.maximum(drawn, -limit), limit).astype(kind)


def setup_inputs(seed: int = 0, part: int = 0) -> dict:
    key_list = jax.random.split(jax.random.key(seed), 7)
    part_keys = jax.random.split(jax.random.fold_in(key_list[6], part), 7)
    query = draw_query(jax.random.fold_in(jax.random.fold_in(key_list[6], part), 71), part)
    key_seq = draw_key_seq(jax.random.fold_in(jax.random.fold_in(key_list[6], part), 71), part)
    value_seq = scatter_about(part_keys[2], (TOKENS, KVH * DH), 1.0, 6.0, ((0, 16),))
    attn_out = scatter_about(part_keys[3], (TOKENS, H * DH), 1.0, 6.0, ((0, 16),))
    grad_out = scatter_about(part_keys[4], (TOKENS, H * DH), 1.0, 6.0, ((0, 16),))
    lse = draw_lse(jax.random.fold_in(jax.random.fold_in(key_list[6], part), 71), part)
    return {"query": query, "key_seq": key_seq, "value_seq": value_seq, "attn_out": attn_out, "grad_out": grad_out, "lse": lse}


def reference(query, key_seq, value_seq, attn_out, grad_out, lse):
    scale_factor = DH ** -0.5
    group_size = H // KVH
    products = grad_out.astype(jnp.float32) * attn_out.astype(jnp.float32)
    delta = products.reshape(TOKENS, H, DH).sum(axis=2).astype(jnp.bfloat16)
    query_heads = query.reshape(TOKENS, H, DH).transpose(1, 0, 2)
    grad_heads = grad_out.reshape(TOKENS, H, DH).transpose(1, 0, 2)
    key_heads = key_seq.reshape(TOKENS, KVH, DH).transpose(1, 0, 2)
    value_heads = value_seq.reshape(TOKENS, KVH, DH).transpose(1, 0, 2)
    row_ids = jnp.arange(TOKENS, dtype=jnp.int32)
    causal = row_ids[:, None] >= row_ids[None, :]

    def one_head(head):
        group = head // group_size
        q_rows = query_heads[head]
        k_rows = key_heads[group]
        v_rows = value_heads[group]
        g_rows = grad_heads[head]
        scores = jnp.dot(q_rows, k_rows.T, preferred_element_type=jnp.float32) * scale_factor
        scores = jnp.where(causal, scores, -1e30)
        probs = jnp.exp(scores - lse[head][:, None])
        probs_low = probs.astype(jnp.bfloat16)
        value_part = jnp.dot(probs_low.T, g_rows, preferred_element_type=jnp.float32)
        grad_probs = jnp.dot(g_rows, v_rows.T, preferred_element_type=jnp.float32)
        delta_col = delta[:, head].astype(jnp.float32)[:, None]
        score_grad = (probs * (grad_probs - delta_col)).astype(jnp.bfloat16)
        query_part = (jnp.dot(score_grad, k_rows, preferred_element_type=jnp.float32) * scale_factor).astype(jnp.bfloat16)
        key_part = jnp.dot(score_grad.T, q_rows, preferred_element_type=jnp.float32) * scale_factor
        return query_part, key_part, value_part

    query_parts, key_parts, value_parts = lax.map(one_head, jnp.arange(H, dtype=jnp.int32))
    query_grad = query_parts.transpose(1, 0, 2).reshape(TOKENS, H * DH)
    key_sum = key_parts.reshape(KVH, group_size, TOKENS, DH).sum(axis=1)
    value_sum = value_parts.reshape(KVH, group_size, TOKENS, DH).sum(axis=1)
    key_grad = key_sum.transpose(1, 0, 2).reshape(TOKENS, KVH * DH).astype(jnp.bfloat16)
    value_grad = value_sum.transpose(1, 0, 2).reshape(TOKENS, KVH * DH).astype(jnp.bfloat16)
    return (query_grad, key_grad, value_grad)
```

```python
import functools

import jax
import jax.numpy as jnp
from jax import lax
from jax.experimental import pallas as pl
from jax.experimental.pallas import tpu as pltpu
from jax.sharding import PartitionSpec as P

DH = 128
SCALE = DH ** (-0.5)
LOG2E = 1.4426950408889634
NT = (((1,), (1,)), ((), ()))
NN = (((1,), (0,)), ((), ()))
VMEM = pl.BlockSpec(memory_space=pltpu.VMEM)
SMEM = pl.BlockSpec(memory_space=pltpu.SMEM)
LIMIT = 56 << 20


def dot(a, b, dims):
    return lax.dot_general(a, b, dims, preferred_element_type=jnp.float32)


def call(body, out_shape, in_specs, out_specs, flops=0, exps=0, **kw):
    return pl.pallas_call(
        body,
        out_shape=out_shape,
        in_specs=in_specs,
        out_specs=out_specs,
        compiler_params=pltpu.CompilerParams(vmem_limit_bytes=LIMIT),
        cost_estimate=pl.CostEstimate(
            flops=flops, transcendentals=exps, bytes_accessed=4 << 20
        ),
        **kw,
    )


def pack(key, value, out, grad, seq_count, kv_heads, heads_here, pad):
    rows = key.shape[0]
    width = heads_here * DH
    group = heads_here * seq_count // kv_heads

    def body(k_ref, v_ref, o_ref, g_ref, grad_ref, kvd_ref):
        for d in range(seq_count):
            grad_ref[d] = g_ref[:, d * width : (d + 1) * width]
        for g in range(kv_heads):
            kvd_ref[g, :rows, :DH] = k_ref[:, g * DH : (g + 1) * DH]
            kvd_ref[g, :rows, DH:] = v_ref[:, g * DH : (g + 1) * DH]
            cols = []
            for h in range(g * group, (g + 1) * group):
                c = slice(h * DH, (h + 1) * DH)
                prod = g_ref[:, c].astype(jnp.float32) * o_ref[:, c].astype(jnp.float32)
                cols.append(jnp.sum(prod, axis=1, keepdims=True))
            cols.append(jnp.zeros((rows, pad - group), jnp.float32))
            delta = jnp.concatenate(cols, axis=1).T
            fill = jnp.zeros((pad, 2 * DH - rows), jnp.float32)
            kvd_ref[g, rows:, :] = jnp.concatenate([delta, fill], axis=1).astype(jnp.bfloat16)

    return call(
        body,
        (
            jax.ShapeDtypeStruct((seq_count, rows, width), jnp.bfloat16),
            jax.ShapeDtypeStruct((kv_heads, rows + pad, 2 * DH), jnp.bfloat16),
        ),
        [VMEM] * 4,
        (VMEM, VMEM),
    )(key, value, out, grad)


def unpack(pos, lse, pieces, rows, heads_here, kv_heads, pad):
    copies = len(pieces)
    total = rows * copies * kv_heads

    def body(pos_ref, lse_ref, *refs):
        ins, (kv_ref, kt_ref, delta_ref, lse_out) = refs[:copies], refs[copies:]
        plane, place = pos_ref[0], pos_ref[1]
        lse_out[...] = lse_ref[...] * LOG2E
        for s in range(copies):
            source = lax.rem(place - s + copies, copies)
            for r in range(kv_heads):
                owner = lax.rem(plane - r + kv_heads, kv_heads) * copies + source
                start = pl.multiple_of(owner * rows, rows)
                kv_ref[pl.ds(start, rows), :] = ins[s][r, :rows, :]
                low = ins[s][r, rows:, :rows].astype(jnp.float32)
                ids = lax.broadcasted_iota(jnp.int32, (pad, rows), 0)
                for h in range(heads_here):
                    mine = ids == place * heads_here + h
                    row = jnp.sum(jnp.where(mine, low, 0.0), axis=0, keepdims=True)
                    delta_ref[h : h + 1, pl.ds(start, rows)] = row
        kt_ref[...] = kv_ref[:, :DH].T

    return call(
        body,
        (
            jax.ShapeDtypeStruct((total, 2 * DH), jnp.bfloat16),
            jax.ShapeDtypeStruct((DH, total), jnp.bfloat16),
            jax.ShapeDtypeStruct((heads_here, total), jnp.float32),
            jax.ShapeDtypeStruct((heads_here, total), jnp.float32),
        ),
        [SMEM, VMEM] + [VMEM] * copies,
        (VMEM,) * 4,
    )(pos, lse, *pieces)


def probs_and_grads(kb, vb, qb, gb, lse, delta, k0, q0):
    s = dot(kb, qb, NT) * (SCALE * LOG2E) - lse
    if k0 + kb.shape[0] > q0:
        key_ids = k0 + lax.broadcasted_iota(jnp.int32, s.shape, 0)
        query_ids = q0 + lax.broadcasted_iota(jnp.int32, s.shape, 1)
        s = jnp.where(key_ids <= query_ids, s, -1e30)
    p = jnp.exp2(s)
    ds = (p * (dot(vb, gb, NT) - delta)).astype(jnp.bfloat16)
    return p, ds


def query_kernel(q, g, kv, kt, lse, delta, bq, bk):
    total = q.shape[0]
    heads = q.shape[1] // DH

    def body(q_ref, g_ref, kv_ref, kt_ref, l_ref, d_ref, o_ref):
        for q0 in range(0, total, bq):
            q1 = q0 + bq
            for h in range(heads):
                c = slice(h * DH, (h + 1) * DH)
                acc = None
                for k0 in range(0, q1, bk):
                    k1 = min(k0 + bk, q1)
                    _, ds = probs_and_grads(
                        kv_ref[k0:k1, :DH],
                        kv_ref[k0:k1, DH:],
                        q_ref[q0:q1, c],
                        g_ref[q0:q1, c],
                        l_ref[h : h + 1, q0:q1],
                        d_ref[h : h + 1, q0:q1],
                        k0,
                        q0,
                    )
                    t = dot(kt_ref[:, k0:k1], ds, NN)
                    acc = t if acc is None else acc + t
                o_ref[q0:q1, c] = (acc * SCALE).T.astype(jnp.bfloat16)

    return call(
        body,
        jax.ShapeDtypeStruct(q.shape, jnp.bfloat16),
        [VMEM] * 6,
        VMEM,
        flops=6 * heads * total * total * DH // 2,
        exps=heads * total * total // 2,
    )(q, g, kv, kt, lse, delta)


def key_kernel(pos, q, g, kv, lse, delta, rows, copies, bq, bk):
    total = q.shape[0]
    heads = q.shape[1] // DH
    planes = total // (rows * copies)

    def body(pos_ref, q_ref, g_ref, kv_ref, l_ref, d_ref, o_ref):
        place = pos_ref[1]
        for k0 in range(0, total, bk):
            k1 = k0 + bk
            dk = dv = None
            for q0 in range(k0, total, bq):
                q1 = q0 + bq
                for h in range(heads):
                    c = slice(h * DH, (h + 1) * DH)
                    qb, gb = q_ref[q0:q1, c], g_ref[q0:q1, c]
                    p, ds = probs_and_grads(
                        kv_ref[k0:k1, :DH],
                        kv_ref[k0:k1, DH:],
                        qb,
                        gb,
                        l_ref[h : h + 1, q0:q1],
                        d_ref[h : h + 1, q0:q1],
                        k0,
                        q0,
                    )
                    t = dot(p.astype(jnp.bfloat16), gb, NN)
                    dv = t if dv is None else dv + t
                    t = dot(ds, qb, NN)
                    dk = t if dk is None else dk + t
            both = jnp.concatenate([dk * SCALE, dv], axis=1).astype(jnp.bfloat16)
            for n in range(bk // rows):
                owner = k0 // rows + n
                slot = lax.rem(owner % copies - place + copies, copies)
                o_ref[slot, owner // copies] = both[n * rows : (n + 1) * rows]

    return call(
        body,
        jax.ShapeDtypeStruct((copies, planes, rows, 2 * DH), jnp.bfloat16),
        [SMEM] + [VMEM] * 5,
        VMEM,
        flops=8 * heads * total * total * DH // 2,
        exps=heads * total * total // 2,
    )(pos, q, g, kv, lse, delta)


def finish_kv(pos, blocks):
    kv_heads = len(blocks)
    rows = blocks[0].shape[0]

    def body(pos_ref, *refs):
        ins, (k_ref, v_ref) = refs[:kv_heads], refs[kv_heads:]
        for r in range(kv_heads):
            g = lax.rem(pos_ref[0] - r + kv_heads, kv_heads)
            cols = pl.ds(pl.multiple_of(g * DH, DH), DH)
            k_ref[:, cols] = ins[r][:, :DH]
            v_ref[:, cols] = ins[r][:, DH:]

    out = jax.ShapeDtypeStruct((rows, kv_heads * DH), jnp.bfloat16)
    return call(body, (out, out), [SMEM] + [VMEM] * kv_heads, (VMEM, VMEM))(pos, *blocks)


def per_device(query, key_seq, value_seq, attn_out, grad_out, lse):
    seq_count = lax.axis_size("seq")
    rows = key_seq.shape[0]
    total = rows * seq_count
    kv_heads = key_seq.shape[1] // DH
    heads_here = lse.shape[0]
    copies = seq_count // kv_heads
    group = heads_here * copies
    pad = -(-group // 16) * 16
    me = lax.axis_index("seq")
    plane, place = me // copies, me % copies
    pos = jnp.stack([plane, place]).astype(jnp.int32)

    def across(x, r):
        turn = [(j, (j + r * copies) % seq_count) for j in range(seq_count)]
        return lax.ppermute(x, "seq", turn)

    def inside(x, s):
        turn = [(j, j // copies * copies + (j + s) % copies) for j in range(seq_count)]
        return lax.ppermute(x, "seq", turn)

    grad_send, kvd = pack(
        key_seq, value_seq, attn_out, grad_out, seq_count, kv_heads, heads_here, pad
    )
    grad = lax.all_to_all(
        grad_send.reshape(total, heads_here * DH), "seq", split_axis=0, concat_axis=0, tiled=True
    )

    def pick(x, n):
        return lax.dynamic_index_in_dim(x, n % x.shape[0], 0, keepdims=False)

    got = [pick(kvd, plane)] + [across(pick(kvd, plane + r), r) for r in range(1, kv_heads)]
    mine = jnp.stack(got)
    pieces = [mine] + [inside(mine, s) for s in range(1, copies)]
    kv, kt, delta, lse2 = unpack(pos, lse, pieces, rows, heads_here, kv_heads, pad)

    big = min(512, total)
    query_local = query_kernel(query, grad, kv, kt, lse2, delta, big, min(1024, total))
    back = lax.all_to_all(query_local, "seq", split_axis=0, concat_axis=0, tiled=True)
    query_grad = (
        back.reshape(seq_count, rows, heads_here * DH)
        .transpose(1, 0, 2)
        .reshape(rows, seq_count * heads_here * DH)
    )
    partial = key_kernel(pos, query, grad, kv, lse2, delta, rows, copies, big, big)
    parts = [partial[0]] + [inside(partial[s], s) for s in range(1, copies)]
    summed = functools.reduce(
        lambda a, b: a + b, (part.astype(jnp.float32) for part in parts)
    ).astype(jnp.bfloat16)
    blocks = [pick(summed, plane)] + [
        across(pick(summed, plane + r), r) for r in range(1, kv_heads)
    ]
    key_grad, value_grad = finish_kv(pos, blocks)
    return query_grad, key_grad, value_grad


def solution(mesh):
    tokens = P(("dp", "seq"), None)
    return jax.shard_map(
        per_device,
        mesh=mesh,
        in_specs=(P("dp", "seq"), tokens, tokens, tokens, tokens, P("seq", "dp")),
        out_specs=(tokens, tokens, tokens),
        check_vma=False,
    )
```

```python
import functools

import jax
import jax.numpy as jnp
from jax import lax
from jax.experimental import pallas as pl
from jax.experimental.pallas import tpu as pltpu
from jax.sharding import PartitionSpec as P

DH = 128
SCALE = DH ** (-0.5)
LOG2E = 1.4426950408889634
NT = (((1,), (1,)), ((), ()))
NN = (((1,), (0,)), ((), ()))
VMEM = pl.BlockSpec(memory_space=pltpu.VMEM)
SMEM = pl.BlockSpec(memory_space=pltpu.SMEM)
LIMIT = 56 << 20


def dot(a, b, dims):
    return lax.dot_general(a, b, dims, preferred_element_type=jnp.float32)


def call(body, out_shape, in_specs, out_specs, flops=0, exps=0, **kw):
    return pl.pallas_call(
        body,
        out_shape=out_shape,
        in_specs=in_specs,
        out_specs=out_specs,
        compiler_params=pltpu.CompilerParams(vmem_limit_bytes=LIMIT),
        cost_estimate=pl.CostEstimate(
            flops=flops, transcendentals=exps, bytes_accessed=4 << 20
        ),
        **kw,
    )


def pack(out, grad, seq_count, heads_here, pad):
    rows = grad.shape[0]
    width = heads_here * DH
    steps = 4 if seq_count % 4 == 0 else 1
    here = seq_count // steps

    def body(o_ref, g_ref, send_ref):
        for d in range(here):
            c = slice(d * width, (d + 1) * width)
            block = g_ref[:, c]
            send_ref[d, :rows] = block
            prod = block.astype(jnp.float32) * o_ref[:, c].astype(jnp.float32)
            sums = [
                jnp.sum(prod[:, h * DH : (h + 1) * DH], axis=1, keepdims=True)
                for h in range(heads_here)
            ]
            sums.append(jnp.zeros((rows, pad - heads_here), jnp.float32))
            delta = jnp.concatenate(sums, axis=1).T
            if width > rows:
                fill = jnp.zeros((pad, width - rows), jnp.float32)
                delta = jnp.concatenate([delta, fill], axis=1)
            send_ref[d, rows:] = delta.astype(jnp.bfloat16)

    many = pl.BlockSpec((rows, here * width), lambda n: (0, n))
    return call(
        body,
        jax.ShapeDtypeStruct((seq_count, rows + pad, width), jnp.bfloat16),
        [many, many],
        pl.BlockSpec((here, rows + pad, width), lambda n: (n, 0, 0)),
        grid=(steps,),
    )(out, grad)


def unpack(pos, lse, pieces):
    copies = len(pieces)
    kv_heads, rows, width = pieces[0].shape
    total = rows * copies * kv_heads

    def body(pos_ref, lse_ref, *refs):
        ins, (kv_ref, kt_ref, lse_out) = refs[:copies], refs[copies:]
        plane, place = pos_ref[0], pos_ref[1]
        lse_out[...] = lse_ref[...] * LOG2E
        for s in range(copies):
            source = lax.rem(place - s + copies, copies)
            for r in range(kv_heads):
                owner = lax.rem(plane - r + kv_heads, kv_heads) * copies + source
                start = pl.multiple_of(owner * rows, rows)
                kv_ref[pl.ds(start, rows), :] = ins[s][r]
        kt_ref[...] = kv_ref[:, :DH].T

    return call(
        body,
        (
            jax.ShapeDtypeStruct((total, width), jnp.bfloat16),
            jax.ShapeDtypeStruct((DH, total), jnp.bfloat16),
            jax.ShapeDtypeStruct(lse.shape, jnp.float32),
        ),
        [SMEM, VMEM] + [VMEM] * copies,
        (VMEM,) * 3,
        flops=int(40e9),
    )(pos, lse, *pieces)


def attend(pos, q, g, kv, kt, lse, rows, copies, block):
    total = q.shape[0]
    width = q.shape[1]
    heads = width // DH
    planes = total // (rows * copies)
    owners = block // rows

    def body(pos_ref, q_ref, g_ref, kv_ref, kt_ref, l_ref, dq_ref, *refs):
        slots, (acc_ref, dkv_ref, d_ref) = refs[:copies], refs[copies:]
        for n in range(total // rows):
            d_ref[:, n * rows : (n + 1) * rows] = g_ref[n, rows:, :rows].astype(jnp.float32)
        for k0 in range(0, total, block):
            k1 = k0 + block
            kb, vb = kv_ref[k0:k1, :DH], kv_ref[k0:k1, DH:]
            dk = dv = None
            for q0 in range(k0, total, block):
                q1 = q0 + block
                n0 = q0 // rows
                for h in range(heads):
                    c = slice(h * DH, (h + 1) * DH)
                    qb = q_ref[q0:q1, c]
                    gb = g_ref[n0 : n0 + owners, :rows, c].reshape(block, DH)
                    s = dot(kb, qb, NT) * (SCALE * LOG2E) - l_ref[h : h + 1, q0:q1]
                    if k1 > q0:
                        key_ids = k0 + lax.broadcasted_iota(jnp.int32, s.shape, 0)
                        query_ids = q0 + lax.broadcasted_iota(jnp.int32, s.shape, 1)
                        s = jnp.where(key_ids <= query_ids, s, -1e30)
                    p = jnp.exp2(s)
                    t = dot(p.astype(jnp.bfloat16), gb, NN)
                    dv = t if dv is None else dv + t
                    ds = p * (dot(vb, gb, NT) - d_ref[h : h + 1, q0:q1])
                    ds = ds.astype(jnp.bfloat16)
                    t = dot(ds, qb, NN)
                    dk = t if dk is None else dk + t
                    t = dot(kt_ref[:, k0:k1], ds, NN)
                    if k0 == 0:
                        acc_ref[c, q0:q1] = t
                    else:
                        acc_ref[c, q0:q1] += t
            dkv_ref[k0:k1, :DH] = (dk * SCALE).astype(jnp.bfloat16)
            dkv_ref[k0:k1, DH:] = dv.astype(jnp.bfloat16)
        for h in range(heads):
            c = slice(h * DH, (h + 1) * DH)
            for q0 in range(0, total, block):
                q1 = q0 + block
                dq_ref[q0:q1, c] = (acc_ref[c, q0:q1] * SCALE).T.astype(jnp.bfloat16)
        for s in range(copies):
            target = lax.rem(pos_ref[1] + s, copies)
            for r in range(planes):
                start = pl.multiple_of((r * copies + target) * rows, rows)
                slots[s][r] = dkv_ref[pl.ds(start, rows), :]

    part = jax.ShapeDtypeStruct((planes, rows, 2 * DH), jnp.bfloat16)
    return call(
        body,
        (jax.ShapeDtypeStruct((total, width), jnp.bfloat16),) + (part,) * copies,
        [SMEM] + [VMEM] * 5,
        (VMEM,) * (1 + copies),
        flops=10 * heads * total * total * DH // 2,
        exps=heads * total * total // 2,
        scratch_shapes=[
            pltpu.VMEM((width, total), jnp.float32),
            pltpu.VMEM((total, 2 * DH), jnp.bfloat16),
            pltpu.VMEM((g.shape[1] - rows, total), jnp.float32),
        ],
    )(pos, q, g, kv, kt, lse)


def finish_kv(pos, blocks):
    kv_heads = len(blocks)
    rows = blocks[0].shape[0]

    def body(pos_ref, *refs):
        ins, (k_ref, v_ref) = refs[:kv_heads], refs[kv_heads:]
        for r in range(kv_heads):
            g = lax.rem(pos_ref[0] - r + kv_heads, kv_heads)
            cols = pl.ds(pl.multiple_of(g * DH, DH), DH)
            k_ref[:, cols] = ins[r][:, :DH]
            v_ref[:, cols] = ins[r][:, DH:]

    out = jax.ShapeDtypeStruct((rows, kv_heads * DH), jnp.bfloat16)
    return call(body, (out, out), [SMEM] + [VMEM] * kv_heads, (VMEM, VMEM), flops=int(16e9))(pos, *blocks)


def per_device(query, key_seq, value_seq, attn_out, grad_out, lse):
    seq_count = lax.axis_size("seq")
    rows = key_seq.shape[0]
    total = rows * seq_count
    kv_heads = key_seq.shape[1] // DH
    heads_here = lse.shape[0]
    copies = seq_count // kv_heads
    pad = -(-heads_here // 8) * 8
    me = lax.axis_index("seq")
    plane, place = me // copies, me % copies
    pos = jnp.stack([plane, place]).astype(jnp.int32)

    def across(x, r):
        turn = [(j, (j + r * copies) % seq_count) for j in range(seq_count)]
        return lax.ppermute(x, "seq", turn)

    def inside(x, s):
        turn = [(j, j // copies * copies + (j + s) % copies) for j in range(seq_count)]
        return lax.ppermute(x, "seq", turn)

    def columns(x, n):
        return lax.dynamic_slice_in_dim(x, n % kv_heads * DH, DH, axis=1)

    def pick(x, n):
        return lax.dynamic_index_in_dim(x, n % x.shape[0], 0, keepdims=False)

    got = []
    for r in range(kv_heads):
        both = jnp.concatenate([columns(key_seq, plane + r), columns(value_seq, plane + r)], axis=1)
        got.append(across(both, r) if r else both)
    mine = jnp.stack(got)
    send = pack(attn_out, grad_out, seq_count, heads_here, pad)
    send, mine = lax.optimization_barrier((send, mine))
    pieces = [mine] + [inside(mine, s) for s in range(1, copies)]
    grad = lax.all_to_all(send, "seq", split_axis=0, concat_axis=0, tiled=True)
    kv, kt, lse2 = unpack(pos, lse, pieces)

    query_local, *parts = attend(pos, query, grad, kv, kt, lse2, rows, copies, min(512, total))
    parts = parts[:1] + [inside(parts[s], s) for s in range(1, copies)]
    back = lax.all_to_all(query_local, "seq", split_axis=0, concat_axis=0, tiled=True)
    query_grad = (
        back.reshape(seq_count, rows, heads_here * DH)
        .transpose(1, 0, 2)
        .reshape(rows, seq_count * heads_here * DH)
    )
    summed = functools.reduce(
        lambda a, b: a + b, (part.astype(jnp.float32) for part in parts)
    ).astype(jnp.bfloat16)
    blocks = [pick(summed, plane)] + [
        across(pick(summed, plane + r), r) for r in range(1, kv_heads)
    ]
    key_grad, value_grad = finish_kv(pos, blocks)
    return query_grad, key_grad, value_grad


def solution(mesh):
    tokens = P(("dp", "seq"), None)
    return jax.shard_map(
        per_device,
        mesh=mesh,
        in_specs=(P("dp", "seq"), tokens, tokens, tokens, tokens, P("seq", "dp")),
        out_specs=(tokens, tokens, tokens),
        check_vma=False,
    )
```

```python
import functools

import jax
import jax.numpy as jnp
from jax import lax
from jax.experimental import pallas as pl
from jax.experimental.pallas import tpu as pltpu
from jax.sharding import PartitionSpec as P

DH = 128
SCALE = DH ** (-0.5)
LOG2E = 1.4426950408889634
NT = (((1,), (1,)), ((), ()))
NN = (((1,), (0,)), ((), ()))
VMEM = pl.BlockSpec(memory_space=pltpu.VMEM)
ANY = pl.BlockSpec(memory_space=pl.ANY)
SMEM = pl.BlockSpec(memory_space=pltpu.SMEM)
LIMIT = 36 << 20


def dot(a, b, dims):
    return lax.dot_general(a, b, dims, preferred_element_type=jnp.float32)


def call(body, out_shape, in_specs, out_specs, flops=0, exps=0, **kw):
    return pl.pallas_call(
        body,
        out_shape=out_shape,
        in_specs=in_specs,
        out_specs=out_specs,
        compiler_params=pltpu.CompilerParams(vmem_limit_bytes=LIMIT),
        cost_estimate=pl.CostEstimate(
            flops=flops, transcendentals=exps, bytes_accessed=4 << 20
        ),
        **kw,
    )


def pack(out, grad, seq_count, heads_here, pad):
    rows = grad.shape[0]
    width = heads_here * DH
    steps = 4 if seq_count % 4 == 0 else 1
    here = seq_count // steps

    def body(o_ref, g_ref, send_ref):
        for d in range(here):
            c = slice(d * width, (d + 1) * width)
            block = g_ref[:, c]
            send_ref[d, :rows] = block
            prod = block.astype(jnp.float32) * o_ref[:, c].astype(jnp.float32)
            sums = [
                jnp.sum(prod[:, h * DH : (h + 1) * DH], axis=1, keepdims=True)
                for h in range(heads_here)
            ]
            sums.append(jnp.zeros((rows, pad - heads_here), jnp.float32))
            delta = jnp.concatenate(sums, axis=1).T
            if width > rows:
                fill = jnp.zeros((pad, width - rows), jnp.float32)
                delta = jnp.concatenate([delta, fill], axis=1)
            send_ref[d, rows:] = delta.astype(jnp.bfloat16)

    many = pl.BlockSpec((rows, here * width), lambda n: (0, n))
    return call(
        body,
        jax.ShapeDtypeStruct((seq_count, rows + pad, width), jnp.bfloat16),
        [many, many],
        pl.BlockSpec((here, rows + pad, width), lambda n: (n, 0, 0)),
        grid=(steps,),
    )(out, grad)


def attend(pos, q, g, lse, pieces, block):
    total, width = q.shape
    heads = width // DH
    copies = len(pieces)
    planes, rows, _ = pieces[0].shape
    owners = block // rows

    def body(pos_ref, q_ref, g_ref, lse_ref, *refs):
        ins, dq_ref, slots = refs[:copies], refs[copies], refs[copies + 1 : 2 * copies + 1]
        kv_ref, kt_ref, l_ref, d_ref, acc_ref, dkv_ref, sems = refs[2 * copies + 1 :]
        plane, place = pos_ref[0], pos_ref[1]
        coming = []
        for s in range(copies):
            source = lax.rem(place - s + copies, copies)
            for r in range(planes):
                owner = lax.rem(plane - r + planes, planes) * copies + source
                start = pl.multiple_of(owner * rows, rows)
                copy = pltpu.make_async_copy(
                    ins[s].at[r], kv_ref.at[pl.ds(start, rows)], sems.at[s, r]
                )
                copy.start()
                coming.append(copy)
        l_ref[...] = lse_ref[...] * LOG2E
        for n in range(total // rows):
            d_ref[:, n * rows : (n + 1) * rows] = g_ref[n, rows:, :rows].astype(jnp.float32)
        for copy in coming:
            copy.wait()
        for k0 in range(0, total, block):
            kt_ref[:, k0 : k0 + block] = kv_ref[k0 : k0 + block, :DH].T
        for k0 in range(0, total, block):
            k1 = k0 + block
            kb, vb = kv_ref[k0:k1, :DH], kv_ref[k0:k1, DH:]
            dk = dv = None
            for q0 in range(k0, total, block):
                q1 = q0 + block
                n0 = q0 // rows
                for h in range(heads):
                    c = slice(h * DH, (h + 1) * DH)
                    qb = q_ref[q0:q1, c]
                    gb = g_ref[n0 : n0 + owners, :rows, c].reshape(block, DH)
                    s = dot(kb, qb, NT) * (SCALE * LOG2E) - l_ref[h : h + 1, q0:q1]
                    if k1 > q0:
                        key_ids = k0 + lax.broadcasted_iota(jnp.int32, s.shape, 0)
                        query_ids = q0 + lax.broadcasted_iota(jnp.int32, s.shape, 1)
                        s = jnp.where(key_ids <= query_ids, s, -1e30)
                    p = jnp.exp2(s)
                    t = dot(p.astype(jnp.bfloat16), gb, NN)
                    dv = t if dv is None else dv + t
                    ds = p * (dot(vb, gb, NT) - d_ref[h : h + 1, q0:q1])
                    ds = ds.astype(jnp.bfloat16)
                    t = dot(ds, qb, NN)
                    dk = t if dk is None else dk + t
                    t = dot(kt_ref[:, k0:k1], ds, NN)
                    if k0 == 0:
                        acc_ref[c, q0:q1] = t
                    else:
                        acc_ref[c, q0:q1] += t
            dkv_ref[k0:k1, :DH] = (dk * SCALE).astype(jnp.bfloat16)
            dkv_ref[k0:k1, DH:] = dv.astype(jnp.bfloat16)
        for h in range(heads):
            c = slice(h * DH, (h + 1) * DH)
            for q0 in range(0, total, block):
                q1 = q0 + block
                dq_ref[q0:q1, c] = (acc_ref[c, q0:q1] * SCALE).T.astype(jnp.bfloat16)
        for s in range(copies):
            target = lax.rem(place + s, copies)
            for r in range(planes):
                start = pl.multiple_of((r * copies + target) * rows, rows)
                slots[s][r] = dkv_ref[pl.ds(start, rows), :]

    part = jax.ShapeDtypeStruct((planes, rows, 2 * DH), jnp.bfloat16)
    return call(
        body,
        (jax.ShapeDtypeStruct((total, width), jnp.bfloat16),) + (part,) * copies,
        [SMEM] + [VMEM] * 3 + [ANY] * copies,
        (VMEM,) * (1 + copies),
        flops=10 * heads * total * total * DH // 2,
        exps=heads * total * total // 2,
        scratch_shapes=[
            pltpu.VMEM((total, 2 * DH), jnp.bfloat16),
            pltpu.VMEM((DH, total), jnp.bfloat16),
            pltpu.VMEM(lse.shape, jnp.float32),
            pltpu.VMEM((g.shape[1] - rows, total), jnp.float32),
            pltpu.VMEM((width, total), jnp.float32),
            pltpu.VMEM((total, 2 * DH), jnp.bfloat16),
            pltpu.SemaphoreType.DMA((copies, planes)),
        ],
    )(pos, q, g, lse, *pieces)


def finish_kv(pos, blocks):
    kv_heads = len(blocks)
    rows = blocks[0].shape[0]

    def body(pos_ref, *refs):
        ins, (k_ref, v_ref) = refs[:kv_heads], refs[kv_heads:]
        for r in range(kv_heads):
            g = lax.rem(pos_ref[0] - r + kv_heads, kv_heads)
            cols = pl.ds(pl.multiple_of(g * DH, DH), DH)
            k_ref[:, cols] = ins[r][:, :DH]
            v_ref[:, cols] = ins[r][:, DH:]

    out = jax.ShapeDtypeStruct((rows, kv_heads * DH), jnp.bfloat16)
    return call(body, (out, out), [SMEM] + [VMEM] * kv_heads, (VMEM, VMEM), flops=int(16e9))(pos, *blocks)


def per_device(query, key_seq, value_seq, attn_out, grad_out, lse):
    seq_count = lax.axis_size("seq")
    rows = key_seq.shape[0]
    total = rows * seq_count
    kv_heads = key_seq.shape[1] // DH
    heads_here = lse.shape[0]
    copies = seq_count // kv_heads
    pad = -(-heads_here // 8) * 8
    me = lax.axis_index("seq")
    plane, place = me // copies, me % copies
    pos = jnp.stack([plane, place]).astype(jnp.int32)

    def across(x, r):
        turn = [(j, (j + r * copies) % seq_count) for j in range(seq_count)]
        return lax.ppermute(x, "seq", turn)

    def inside(x, s):
        turn = [(j, j // copies * copies + (j + s) % copies) for j in range(seq_count)]
        return lax.ppermute(x, "seq", turn)

    def columns(x, n):
        return lax.dynamic_slice_in_dim(x, n % kv_heads * DH, DH, axis=1)

    def pick(x, n):
        return lax.dynamic_index_in_dim(x, n % x.shape[0], 0, keepdims=False)

    got = []
    for r in range(kv_heads):
        both = jnp.concatenate([columns(key_seq, plane + r), columns(value_seq, plane + r)], axis=1)
        got.append(across(both, r) if r else both)
    mine = jnp.stack(got)
    send = pack(attn_out, grad_out, seq_count, heads_here, pad)
    send, mine = lax.optimization_barrier((send, mine))
    pieces = [mine] + [inside(mine, s) for s in range(1, copies)]
    grad = lax.all_to_all(send, "seq", split_axis=0, concat_axis=0, tiled=True)
    pieces = [pltpu.with_memory_space_constraint(x, pltpu.HBM) for x in pieces]
    query_local, *parts = attend(pos, query, grad, lse, pieces, min(512, total))
    parts = parts[:1] + [inside(parts[s], s) for s in range(1, copies)]
    back = lax.all_to_all(query_local, "seq", split_axis=0, concat_axis=0, tiled=True)
    query_grad = (
        back.reshape(seq_count, rows, heads_here * DH)
        .transpose(1, 0, 2)
        .reshape(rows, seq_count * heads_here * DH)
    )
    summed = functools.reduce(
        lambda a, b: a + b, (part.astype(jnp.float32) for part in parts)
    ).astype(jnp.bfloat16)
    blocks = [pick(summed, plane)] + [
        across(pick(summed, plane + r), r) for r in range(1, kv_heads)
    ]
    key_grad, value_grad = finish_kv(pos, blocks)
    return query_grad, key_grad, value_grad


def solution(mesh):
    tokens = P(("dp", "seq"), None)
    return jax.shard_map(
        per_device,
        mesh=mesh,
        in_specs=(P("dp", "seq"), tokens, tokens, tokens, tokens, P("seq", "dp")),
        out_specs=(tokens, tokens, tokens),
        check_vma=False,
    )
```

```python
import jax
import jax.numpy as jnp
from jax import lax
from jax.experimental import pallas as pl
from jax.experimental.pallas import tpu as pltpu
from jax.sharding import PartitionSpec as P

DH = 128
SCALE = DH ** (-0.5)
LOG2E = 1.4426950408889634
NT = (((1,), (1,)), ((), ()))
NN = (((1,), (0,)), ((), ()))
VMEM = pl.BlockSpec(memory_space=pltpu.VMEM)
ANY = pl.BlockSpec(memory_space=pl.ANY)
SMEM = pl.BlockSpec(memory_space=pltpu.SMEM)
LIMIT = 36 << 20


def dot(a, b, dims):
    return lax.dot_general(a, b, dims, preferred_element_type=jnp.float32)


def call(body, out_shape, in_specs, out_specs, flops=0, exps=0, **kw):
    return pl.pallas_call(
        body,
        out_shape=out_shape,
        in_specs=in_specs,
        out_specs=out_specs,
        compiler_params=pltpu.CompilerParams(vmem_limit_bytes=LIMIT),
        cost_estimate=pl.CostEstimate(
            flops=flops, transcendentals=exps, bytes_accessed=4 << 20
        ),
        **kw,
    )


def pack(out, grad, seq_count, heads_here, pad):
    rows = grad.shape[0]
    width = heads_here * DH
    cols = 4 * width if seq_count % 4 == 0 else width
    here = cols // width

    def body(o_ref, g_ref, send_ref):
        at = lax.broadcasted_iota(jnp.int32, (cols, 128), 0) // DH
        at = at // heads_here * pad + at % heads_here
        ones = (at == lax.broadcasted_iota(jnp.int32, (cols, 128), 1)).astype(jnp.bfloat16)
        for n in range(0, seq_count, here):
            c = slice(n * width, n * width + cols)
            prod = g_ref[:, c].astype(jnp.float32) * o_ref[:, c].astype(jnp.float32)
            high = prod.astype(jnp.bfloat16)
            low = (prod - high.astype(jnp.float32)).astype(jnp.bfloat16)
            delta = (dot(high, ones, NN) + dot(low, ones, NN)).T
            if width > rows:
                fill = jnp.zeros((128, width - rows), jnp.float32)
                delta = jnp.concatenate([delta, fill], axis=1)
            for d in range(here):
                send_ref[n + d, :rows] = g_ref[:, (n + d) * width : (n + d + 1) * width]
                send_ref[n + d, rows:] = delta[d * pad : (d + 1) * pad].astype(jnp.bfloat16)

    return call(
        body,
        jax.ShapeDtypeStruct((seq_count, rows + pad, width), jnp.bfloat16),
        [VMEM, VMEM],
        VMEM,
    )(out, grad)


def attend(pos, q, g, lse, pieces, block):
    total, width = q.shape
    heads = width // DH
    copies = len(pieces)
    planes, rows, _ = pieces[0].shape
    owners = block // rows

    def body(pos_ref, q_ref, g_ref, lse_ref, *refs):
        ins, dq_ref, slots = refs[:copies], refs[copies], refs[copies + 1 : 2 * copies + 1]
        kv_ref, kt_ref, l_ref, d_ref, acc_ref, dkv_ref, sems = refs[2 * copies + 1 :]
        plane, place = pos_ref[0], pos_ref[1]
        coming = []
        for s in range(copies):
            source = lax.rem(place - s + copies, copies)
            for r in range(planes):
                owner = lax.rem(plane - r + planes, planes) * copies + source
                start = pl.multiple_of(owner * rows, rows)
                copy = pltpu.make_async_copy(
                    ins[s].at[r], kv_ref.at[pl.ds(start, rows)], sems.at[s, r]
                )
                copy.start()
                coming.append(copy)
        l_ref[...] = lse_ref[...] * LOG2E
        for n in range(total // rows):
            d_ref[:, n * rows : (n + 1) * rows] = g_ref[n, rows:, :rows].astype(jnp.float32)
        for copy in coming:
            copy.wait()
        for k0 in range(0, total, block):
            kt_ref[:, k0 : k0 + block] = kv_ref[k0 : k0 + block, :DH].T
        for k0 in range(0, total, block):
            k1 = k0 + block
            kb, vb = kv_ref[k0:k1, :DH], kv_ref[k0:k1, DH:]
            dk = dv = None
            for q0 in range(k0, total, block):
                q1 = q0 + block
                n0 = q0 // rows
                for h in range(heads):
                    c = slice(h * DH, (h + 1) * DH)
                    qb = q_ref[q0:q1, c]
                    gb = g_ref[n0 : n0 + owners, :rows, c].reshape(block, DH)
                    s = dot(kb, qb, NT) * (SCALE * LOG2E) - l_ref[h : h + 1, q0:q1]
                    if k1 > q0:
                        key_ids = k0 + lax.broadcasted_iota(jnp.int32, s.shape, 0)
                        query_ids = q0 + lax.broadcasted_iota(jnp.int32, s.shape, 1)
                        s = jnp.where(key_ids <= query_ids, s, -1e30)
                    p = jnp.exp2(s)
                    t = dot(p.astype(jnp.bfloat16), gb, NN)
                    dv = t if dv is None else dv + t
                    ds = p * (dot(vb, gb, NT) - d_ref[h : h + 1, q0:q1])
                    ds = ds.astype(jnp.bfloat16)
                    t = dot(ds, qb, NN)
                    dk = t if dk is None else dk + t
                    t = dot(kt_ref[:, k0:k1], ds, NN)
                    if k0 == 0:
                        acc_ref[c, q0:q1] = t
                    else:
                        acc_ref[c, q0:q1] += t
            dkv_ref[k0:k1, :DH] = (dk * SCALE).astype(jnp.bfloat16)
            dkv_ref[k0:k1, DH:] = dv.astype(jnp.bfloat16)
        for h in range(heads):
            c = slice(h * DH, (h + 1) * DH)
            for q0 in range(0, total, block):
                q1 = q0 + block
                dq_ref[q0:q1, c] = (acc_ref[c, q0:q1] * SCALE).T.astype(jnp.bfloat16)
        for s in range(copies):
            target = lax.rem(place + s, copies)
            for r in range(planes):
                start = pl.multiple_of((r * copies + target) * rows, rows)
                slots[s][r] = dkv_ref[pl.ds(start, rows), :]

    part = jax.ShapeDtypeStruct((planes, rows, 2 * DH), jnp.bfloat16)
    return call(
        body,
        (jax.ShapeDtypeStruct((total, width), jnp.bfloat16),) + (part,) * copies,
        [SMEM] + [VMEM] * 3 + [ANY] * copies,
        (VMEM,) * (1 + copies),
        flops=10 * heads * total * total * DH // 2,
        exps=heads * total * total // 2,
        scratch_shapes=[
            pltpu.VMEM((total, 2 * DH), jnp.bfloat16),
            pltpu.VMEM((DH, total), jnp.bfloat16),
            pltpu.VMEM(lse.shape, jnp.float32),
            pltpu.VMEM((g.shape[1] - rows, total), jnp.float32),
            pltpu.VMEM((width, total), jnp.float32),
            pltpu.VMEM((total, 2 * DH), jnp.bfloat16),
            pltpu.SemaphoreType.DMA((copies, planes)),
        ],
    )(pos, q, g, lse, *pieces)


def reduce_kv(pos, parts):
    planes, rows, width = parts[0].shape

    def body(pos_ref, *refs):
        ins, outs = refs[: len(parts)], refs[len(parts) :]
        for r in range(planes):
            n = lax.rem(pos_ref[0] + r, planes)
            total = ins[0][n].astype(jnp.float32)
            for part in ins[1:]:
                total = total + part[n].astype(jnp.float32)
            outs[r][...] = total.astype(jnp.bfloat16)

    out = jax.ShapeDtypeStruct((rows, width), jnp.bfloat16)
    return call(
        body,
        (out,) * planes,
        [SMEM] + [VMEM] * len(parts),
        (VMEM,) * planes,
        flops=int(40e9),
    )(pos, *parts)


def finish_kv(pos, blocks, after):
    kv_heads = len(blocks)
    rows = blocks[0].shape[0]

    def body(pos_ref, *refs):
        ins, (_, k_ref, v_ref) = refs[:kv_heads], refs[kv_heads:]
        for r in range(kv_heads):
            g = lax.rem(pos_ref[0] - r + kv_heads, kv_heads)
            cols = pl.ds(pl.multiple_of(g * DH, DH), DH)
            k_ref[:, cols] = ins[r][:, :DH]
            v_ref[:, cols] = ins[r][:, DH:]

    out = jax.ShapeDtypeStruct((rows, kv_heads * DH), jnp.bfloat16)
    return call(body, (out, out), [SMEM] + [VMEM] * kv_heads + [ANY], (VMEM, VMEM))(
        pos, *blocks, after
    )


def per_device(query, key_seq, value_seq, attn_out, grad_out, lse):
    seq_count = lax.axis_size("seq")
    rows = key_seq.shape[0]
    total = rows * seq_count
    kv_heads = key_seq.shape[1] // DH
    heads_here = lse.shape[0]
    copies = seq_count // kv_heads
    pad = -(-heads_here // 8) * 8
    me = lax.axis_index("seq")
    plane, place = me // copies, me % copies
    pos = jnp.stack([plane, place]).astype(jnp.int32)

    def across(x, r):
        turn = [(j, (j + r * copies) % seq_count) for j in range(seq_count)]
        return lax.ppermute(x, "seq", turn)

    def inside(x, s):
        turn = [(j, j // copies * copies + (j + s) % copies) for j in range(seq_count)]
        return lax.ppermute(x, "seq", turn)

    def columns(x, n):
        return lax.dynamic_slice_in_dim(x, n % kv_heads * DH, DH, axis=1)

    def pick(x, n):
        return lax.dynamic_index_in_dim(x, n % x.shape[0], 0, keepdims=False)

    got = []
    for r in range(kv_heads):
        both = jnp.concatenate([columns(key_seq, plane + r), columns(value_seq, plane + r)], axis=1)
        got.append(across(both, r) if r else both)
    mine = jnp.stack(got)
    send = pack(attn_out, grad_out, seq_count, heads_here, pad)
    send, mine = lax.optimization_barrier((send, mine))
    pieces = [mine] + [inside(mine, s) for s in range(1, copies)]
    grad = lax.all_to_all(send, "seq", split_axis=0, concat_axis=0, tiled=True)
    pieces = [pltpu.with_memory_space_constraint(x, pltpu.HBM) for x in pieces]
    query_local, *parts = attend(pos, query, grad, lse, pieces, min(512, total))
    parts = parts[:1] + [inside(parts[s], s) for s in range(1, copies)]
    back = lax.all_to_all(query_local, "seq", split_axis=0, concat_axis=0, tiled=True)
    query_grad = (
        back.reshape(seq_count, rows, heads_here * DH)
        .transpose(1, 0, 2)
        .reshape(rows, seq_count * heads_here * DH)
    )
    sums = reduce_kv(pos, parts)
    blocks = [sums[0]] + [across(sums[r], r) for r in range(1, kv_heads)]
    key_grad, value_grad = finish_kv(pos, blocks, query_grad)
    return query_grad, key_grad, value_grad


def solution(mesh):
    tokens = P(("dp", "seq"), None)
    return jax.shard_map(
        per_device,
        mesh=mesh,
        in_specs=(P("dp", "seq"), tokens, tokens, tokens, tokens, P("seq", "dp")),
        out_specs=(tokens, tokens, tokens),
        check_vma=False,
    )
```

```python
import jax
import jax.numpy as jnp
from jax import lax
from jax.experimental import pallas as pl
from jax.experimental.pallas import tpu as pltpu
from jax.sharding import PartitionSpec as P

DH = 128
SCALE = DH ** (-0.5)
LOG2E = 1.4426950408889634
NT = (((1,), (1,)), ((), ()))
NN = (((1,), (0,)), ((), ()))
VMEM = pl.BlockSpec(memory_space=pltpu.VMEM)
ANY = pl.BlockSpec(memory_space=pl.ANY)
SMEM = pl.BlockSpec(memory_space=pltpu.SMEM)
LIMIT = 36 << 20


def dot(a, b, dims):
    return lax.dot_general(a, b, dims, preferred_element_type=jnp.float32)


def call(body, out_shape, in_specs, out_specs, flops=0, exps=0, **kw):
    return pl.pallas_call(
        body,
        out_shape=out_shape,
        in_specs=in_specs,
        out_specs=out_specs,
        compiler_params=pltpu.CompilerParams(vmem_limit_bytes=LIMIT),
        cost_estimate=pl.CostEstimate(
            flops=flops, transcendentals=exps, bytes_accessed=4 << 20
        ),
        **kw,
    )


def pack(out, grad, seq_count, heads_here, pad):
    rows = grad.shape[0]
    width = heads_here * DH
    cols = 4 * width if seq_count % 4 == 0 else width
    here = cols // width

    def body(o_ref, g_ref, send_ref):
        at = lax.broadcasted_iota(jnp.int32, (cols, 128), 0) // DH
        at = at // heads_here * pad + at % heads_here
        ones = (at == lax.broadcasted_iota(jnp.int32, (cols, 128), 1)).astype(jnp.bfloat16)
        for n in range(0, seq_count, here):
            c = slice(n * width, n * width + cols)
            prod = g_ref[:, c].astype(jnp.float32) * o_ref[:, c].astype(jnp.float32)
            high = prod.astype(jnp.bfloat16)
            low = (prod - high.astype(jnp.float32)).astype(jnp.bfloat16)
            delta = (dot(high, ones, NN) + dot(low, ones, NN)).T
            if DH > rows:
                fill = jnp.zeros((128, DH - rows), jnp.float32)
                delta = jnp.concatenate([delta, fill], axis=1)
            for d in range(here):
                for h in range(heads_here):
                    c = slice((n + d) * width + h * DH, (n + d) * width + (h + 1) * DH)
                    send_ref[n + d, h * rows : (h + 1) * rows] = g_ref[:, c]
                low = delta[d * pad : (d + 1) * pad].astype(jnp.bfloat16)
                send_ref[n + d, heads_here * rows :] = low

    return call(
        body,
        jax.ShapeDtypeStruct((seq_count, heads_here * rows + pad, DH), jnp.bfloat16),
        [VMEM, VMEM],
        VMEM,
    )(out, grad)


def attend(pos, q, g, lse, pieces, block):
    total, width = q.shape
    heads = width // DH
    copies = len(pieces)
    planes, rows, _ = pieces[0].shape
    owners = block // rows

    def body(pos_ref, q_ref, g_ref, lse_ref, *refs):
        ins, dq_ref, slots = refs[:copies], refs[copies], refs[copies + 1 : 2 * copies + 1]
        kv_ref, kt_ref, l_ref, d_ref, acc_ref, dkv_ref, sems = refs[2 * copies + 1 :]
        plane, place = pos_ref[0], pos_ref[1]
        coming = []
        for s in range(copies):
            source = lax.rem(place - s + copies, copies)
            for r in range(planes):
                owner = lax.rem(plane - r + planes, planes) * copies + source
                start = pl.multiple_of(owner * rows, rows)
                copy = pltpu.make_async_copy(
                    ins[s].at[r], kv_ref.at[pl.ds(start, rows)], sems.at[s, r]
                )
                copy.start()
                coming.append(copy)
        l_ref[...] = lse_ref[...] * LOG2E
        for n in range(total // rows):
            d_ref[:, n * rows : (n + 1) * rows] = g_ref[n, heads * rows :, :rows].astype(jnp.float32)
        for copy in coming:
            copy.wait()
        for k0 in range(0, total, block):
            kt_ref[:, k0 : k0 + block] = kv_ref[k0 : k0 + block, :DH].T
        for k0 in range(0, total, block):
            k1 = k0 + block
            kb, vb = kv_ref[k0:k1, :DH], kv_ref[k0:k1, DH:]
            dk = dv = None
            for q0 in range(k0, total, block):
                q1 = q0 + block
                n0 = q0 // rows
                for h in range(heads):
                    c = slice(h * DH, (h + 1) * DH)
                    qb = q_ref[q0:q1, c]
                    gb = g_ref[n0 : n0 + owners, h * rows : (h + 1) * rows].reshape(block, DH)
                    s = dot(kb, qb, NT) * (SCALE * LOG2E) - l_ref[h : h + 1, q0:q1]
                    if k1 > q0:
                        key_ids = k0 + lax.broadcasted_iota(jnp.int32, s.shape, 0)
                        query_ids = q0 + lax.broadcasted_iota(jnp.int32, s.shape, 1)
                        s = jnp.where(key_ids <= query_ids, s, -1e30)
                    p = jnp.exp2(s)
                    t = dot(p.astype(jnp.bfloat16), gb, NN)
                    dv = t if dv is None else dv + t
                    ds = p * (dot(vb, gb, NT) - d_ref[h : h + 1, q0:q1])
                    ds = ds.astype(jnp.bfloat16)
                    t = dot(ds, qb, NN)
                    dk = t if dk is None else dk + t
                    t = dot(kt_ref[:, k0:k1], ds, NN)
                    if k0 == 0:
                        acc_ref[c, q0:q1] = t
                    else:
                        acc_ref[c, q0:q1] += t
                    if q0 == k0:
                        done = (acc_ref[c, q0:q1] * SCALE).astype(jnp.bfloat16)
                        dq_ref[q0:q1, c] = done.T
            dkv_ref[k0:k1, :DH] = (dk * SCALE).astype(jnp.bfloat16)
            dkv_ref[k0:k1, DH:] = dv.astype(jnp.bfloat16)
        for s in range(copies):
            target = lax.rem(place + s, copies)
            for r in range(planes):
                start = pl.multiple_of((r * copies + target) * rows, rows)
                slots[s][r] = dkv_ref[pl.ds(start, rows), :]

    part = jax.ShapeDtypeStruct((planes, rows, 2 * DH), jnp.bfloat16)
    return call(
        body,
        (jax.ShapeDtypeStruct((total, width), jnp.bfloat16),) + (part,) * copies,
        [SMEM] + [VMEM] * 3 + [ANY] * copies,
        (VMEM,) * (1 + copies),
        flops=10 * heads * total * total * DH // 2,
        exps=heads * total * total // 2,
        scratch_shapes=[
            pltpu.VMEM((total, 2 * DH), jnp.bfloat16),
            pltpu.VMEM((DH, total), jnp.bfloat16),
            pltpu.VMEM(lse.shape, jnp.float32),
            pltpu.VMEM((g.shape[1] - heads * rows, total), jnp.float32),
            pltpu.VMEM((width, total), jnp.float32),
            pltpu.VMEM((total, 2 * DH), jnp.bfloat16),
            pltpu.SemaphoreType.DMA((copies, planes)),
        ],
    )(pos, q, g, lse, *pieces)


def stack(blocks):
    def body(*refs):
        for n, ref in enumerate(refs[:-1]):
            refs[-1][n] = ref[...]

    out = jax.ShapeDtypeStruct((len(blocks),) + blocks[0].shape, jnp.bfloat16)
    return call(body, out, [VMEM] * len(blocks), VMEM, flops=int(20e9))(*blocks)


def reduce_kv(pos, parts):
    planes, rows, width = parts[0].shape

    def body(pos_ref, *refs):
        ins, outs = refs[: len(parts)], refs[len(parts) :]
        for r in range(planes):
            n = lax.rem(pos_ref[0] + r, planes)
            total = ins[0][n].astype(jnp.float32)
            for part in ins[1:]:
                total = total + part[n].astype(jnp.float32)
            outs[r][...] = total.astype(jnp.bfloat16)

    out = jax.ShapeDtypeStruct((rows, width), jnp.bfloat16)
    return call(
        body,
        (out,) * planes,
        [SMEM] + [VMEM] * len(parts),
        (VMEM,) * planes,
        flops=int(40e9),
    )(pos, *parts)


def finish_kv(pos, blocks, after):
    kv_heads = len(blocks)
    rows = blocks[0].shape[0]

    def body(pos_ref, *refs):
        ins, (_, k_ref, v_ref) = refs[:kv_heads], refs[kv_heads:]
        for r in range(kv_heads):
            g = lax.rem(pos_ref[0] - r + kv_heads, kv_heads)
            cols = pl.ds(pl.multiple_of(g * DH, DH), DH)
            k_ref[:, cols] = ins[r][:, :DH]
            v_ref[:, cols] = ins[r][:, DH:]

    out = jax.ShapeDtypeStruct((rows, kv_heads * DH), jnp.bfloat16)
    return call(body, (out, out), [SMEM] + [VMEM] * kv_heads + [ANY], (VMEM, VMEM))(
        pos, *blocks, after
    )


def per_device(query, key_seq, value_seq, attn_out, grad_out, lse):
    seq_count = lax.axis_size("seq")
    rows = key_seq.shape[0]
    total = rows * seq_count
    kv_heads = key_seq.shape[1] // DH
    heads_here = lse.shape[0]
    copies = seq_count // kv_heads
    pad = -(-heads_here // 8) * 8
    me = lax.axis_index("seq")
    plane, place = me // copies, me % copies
    pos = jnp.stack([plane, place]).astype(jnp.int32)

    def across(x, r):
        turn = [(j, (j + r * copies) % seq_count) for j in range(seq_count)]
        return lax.ppermute(x, "seq", turn)

    def inside(x, s):
        turn = [(j, j // copies * copies + (j + s) % copies) for j in range(seq_count)]
        return lax.ppermute(x, "seq", turn)

    def columns(x, n):
        return lax.dynamic_slice_in_dim(x, n % kv_heads * DH, DH, axis=1)

    def pick(x, n):
        return lax.dynamic_index_in_dim(x, n % x.shape[0], 0, keepdims=False)

    got = []
    for r in range(kv_heads):
        both = jnp.concatenate([columns(key_seq, plane + r), columns(value_seq, plane + r)], axis=1)
        got.append(across(both, r) if r else both)
    mine = stack(got)
    send = pack(attn_out, grad_out, seq_count, heads_here, pad)
    pieces = [mine] + [inside(mine, s) for s in range(1, copies)]
    grad = lax.all_to_all(send, "seq", split_axis=0, concat_axis=0, tiled=True)
    pieces = [pltpu.with_memory_space_constraint(x, pltpu.HBM) for x in pieces]
    query_local, *parts = attend(pos, query, grad, lse, pieces, min(512, total))
    parts = parts[:1] + [inside(parts[s], s) for s in range(1, copies)]
    back = lax.all_to_all(query_local, "seq", split_axis=0, concat_axis=0, tiled=True)
    query_grad = (
        back.reshape(seq_count, rows, heads_here * DH)
        .transpose(1, 0, 2)
        .reshape(rows, seq_count * heads_here * DH)
    )
    sums = reduce_kv(pos, parts)
    blocks = [sums[0]] + [across(sums[r], r) for r in range(1, kv_heads)]
    key_grad, value_grad = finish_kv(pos, blocks, query_grad)
    return query_grad, key_grad, value_grad


def solution(mesh):
    tokens = P(("dp", "seq"), None)
    return jax.shard_map(
        per_device,
        mesh=mesh,
        in_specs=(P("dp", "seq"), tokens, tokens, tokens, tokens, P("seq", "dp")),
        out_specs=(tokens, tokens, tokens),
        check_vma=False,
    )
```

```python
import jax
import jax.numpy as jnp
from jax import lax
from jax.experimental import pallas as pl
from jax.experimental.pallas import tpu as pltpu
from jax.sharding import PartitionSpec as P

DH = 128
SCALE = DH ** (-0.5)
LOG2E = 1.4426950408889634
NT = (((1,), (1,)), ((), ()))
NN = (((1,), (0,)), ((), ()))
VMEM = pl.BlockSpec(memory_space=pltpu.VMEM)
ANY = pl.BlockSpec(memory_space=pl.ANY)
SMEM = pl.BlockSpec(memory_space=pltpu.SMEM)
LIMIT = 36 << 20


def dot(a, b, dims):
    return lax.dot_general(a, b, dims, preferred_element_type=jnp.float32)


def call(body, out_shape, in_specs, out_specs, flops=0, exps=0, **kw):
    return pl.pallas_call(
        body,
        out_shape=out_shape,
        in_specs=in_specs,
        out_specs=out_specs,
        compiler_params=pltpu.CompilerParams(vmem_limit_bytes=LIMIT),
        cost_estimate=pl.CostEstimate(
            flops=flops, transcendentals=exps, bytes_accessed=4 << 20
        ),
        **kw,
    )


def pack(out, grad, seq_count, heads_here, pad):
    rows = grad.shape[0]
    width = heads_here * DH
    cols = 4 * width if seq_count % 4 == 0 else width
    here = cols // width

    def body(o_ref, g_ref, send_ref):
        at = lax.broadcasted_iota(jnp.int32, (cols, 128), 0) // DH
        at = at // heads_here * pad + at % heads_here
        ones = (at == lax.broadcasted_iota(jnp.int32, (cols, 128), 1)).astype(jnp.bfloat16)
        for n in range(0, seq_count, here):
            c = slice(n * width, n * width + cols)
            prod = g_ref[:, c].astype(jnp.float32) * o_ref[:, c].astype(jnp.float32)
            high = prod.astype(jnp.bfloat16)
            low = (prod - high.astype(jnp.float32)).astype(jnp.bfloat16)
            delta = (dot(high, ones, NN) + dot(low, ones, NN)).T
            if DH > rows:
                fill = jnp.zeros((128, DH - rows), jnp.float32)
                delta = jnp.concatenate([delta, fill], axis=1)
            for d in range(here):
                for h in range(heads_here):
                    c = slice((n + d) * width + h * DH, (n + d) * width + (h + 1) * DH)
                    send_ref[n + d, h * rows : (h + 1) * rows] = g_ref[:, c]
                low = delta[d * pad : (d + 1) * pad].astype(jnp.bfloat16)
                send_ref[n + d, heads_here * rows :] = low

    return call(
        body,
        jax.ShapeDtypeStruct((seq_count, heads_here * rows + pad, DH), jnp.bfloat16),
        [VMEM, VMEM],
        VMEM,
    )(out, grad)


def attend(pos, q, g, lse, pieces, block):
    total, width = q.shape
    heads = width // DH
    copies = len(pieces)
    planes, rows, _ = pieces[0].shape
    owners = block // rows

    def body(pos_ref, q_ref, g_ref, lse_ref, *refs):
        ins, dq_ref, slots = refs[:copies], refs[copies], refs[copies + 1 : 2 * copies + 1]
        kv_ref, l_ref, d_ref, acc_ref, dkv_ref, sems = refs[2 * copies + 1 :]
        plane, place = pos_ref[0], pos_ref[1]
        coming = []
        for s in range(copies):
            if copies & (copies - 1):
                source = lax.rem(place - s + copies, copies)
            else:
                source = place ^ s
            for r in range(planes):
                owner = lax.rem(plane - r + planes, planes) * copies + source
                start = pl.multiple_of(owner * rows, rows)
                copy = pltpu.make_async_copy(
                    ins[s].at[r], kv_ref.at[pl.ds(start, rows)], sems.at[s, r]
                )
                copy.start()
                coming.append(copy)
        l_ref[...] = lse_ref[...] * LOG2E
        for n in range(total // rows):
            d_ref[:, n * rows : (n + 1) * rows] = g_ref[n, heads * rows :, :rows].astype(jnp.float32)
        for copy in coming:
            copy.wait()
        for k0 in range(0, total, block):
            k1 = k0 + block
            kb, vb = kv_ref[k0:k1, :DH], kv_ref[k0:k1, DH:]
            kt = kb.T
            dk = dv = None
            for q0 in range(k0, total, block):
                q1 = q0 + block
                n0 = q0 // rows
                for h in range(heads):
                    c = slice(h * DH, (h + 1) * DH)
                    qb = q_ref[q0:q1, c]
                    gb = g_ref[n0 : n0 + owners, h * rows : (h + 1) * rows].reshape(block, DH)
                    s = dot(kb, qb, NT) * (SCALE * LOG2E) - l_ref[h : h + 1, q0:q1]
                    if k1 > q0:
                        key_ids = k0 + lax.broadcasted_iota(jnp.int32, s.shape, 0)
                        query_ids = q0 + lax.broadcasted_iota(jnp.int32, s.shape, 1)
                        s = jnp.where(key_ids <= query_ids, s, -1e30)
                    p = jnp.exp2(s)
                    t = dot(p.astype(jnp.bfloat16), gb, NN)
                    dv = t if dv is None else dv + t
                    ds = p * (dot(vb, gb, NT) - d_ref[h : h + 1, q0:q1])
                    ds = ds.astype(jnp.bfloat16)
                    t = dot(ds, qb, NN)
                    dk = t if dk is None else dk + t
                    t = dot(kt, ds, NN)
                    if k0 == 0:
                        acc_ref[c, q0:q1] = t
                    else:
                        acc_ref[c, q0:q1] += t
                    if q0 == k0:
                        done = (acc_ref[c, q0:q1] * SCALE).astype(jnp.bfloat16)
                        dq_ref[q0:q1, c] = done.T
            dkv_ref[k0:k1, :DH] = (dk * SCALE).astype(jnp.bfloat16)
            dkv_ref[k0:k1, DH:] = dv.astype(jnp.bfloat16)
        for s in range(copies):
            target = lax.rem(place + s, copies)
            for r in range(planes):
                start = pl.multiple_of((r * copies + target) * rows, rows)
                slots[s][r] = dkv_ref[pl.ds(start, rows), :]

    part = jax.ShapeDtypeStruct((planes, rows, 2 * DH), jnp.bfloat16)
    return call(
        body,
        (jax.ShapeDtypeStruct((total, width), jnp.bfloat16),) + (part,) * copies,
        [SMEM] + [VMEM] * 3 + [ANY] * copies,
        (VMEM,) * (1 + copies),
        flops=10 * heads * total * total * DH // 2,
        exps=heads * total * total // 2,
        scratch_shapes=[
            pltpu.VMEM((total, 2 * DH), jnp.bfloat16),
            pltpu.VMEM(lse.shape, jnp.float32),
            pltpu.VMEM((g.shape[1] - heads * rows, total), jnp.float32),
            pltpu.VMEM((width, total), jnp.float32),
            pltpu.VMEM((total, 2 * DH), jnp.bfloat16),
            pltpu.SemaphoreType.DMA((copies, planes)),
        ],
    )(pos, q, g, lse, *pieces)


def stack(blocks):
    def body(*refs):
        for n, ref in enumerate(refs[:-1]):
            refs[-1][n] = ref[...]

    out = jax.ShapeDtypeStruct((len(blocks),) + blocks[0].shape, jnp.bfloat16)
    return call(body, out, [VMEM] * len(blocks), VMEM, flops=int(20e9))(*blocks)


def reduce_kv(pos, parts):
    planes, rows, width = parts[0].shape

    def body(pos_ref, *refs):
        ins, outs = refs[: len(parts)], refs[len(parts) :]
        for r in range(planes):
            n = lax.rem(pos_ref[0] + r, planes)
            total = ins[0][n].astype(jnp.float32)
            for part in ins[1:]:
                total = total + part[n].astype(jnp.float32)
            outs[r][...] = total.astype(jnp.bfloat16)

    out = jax.ShapeDtypeStruct((rows, width), jnp.bfloat16)
    return call(
        body,
        (out,) * planes,
        [SMEM] + [VMEM] * len(parts),
        (VMEM,) * planes,
        flops=int(40e9),
    )(pos, *parts)


def finish_kv(pos, blocks, after):
    kv_heads = len(blocks)
    rows = blocks[0].shape[0]

    def body(pos_ref, *refs):
        ins, (_, k_ref, v_ref) = refs[:kv_heads], refs[kv_heads:]
        for r in range(kv_heads):
            g = lax.rem(pos_ref[0] - r + kv_heads, kv_heads)
            cols = pl.ds(pl.multiple_of(g * DH, DH), DH)
            k_ref[:, cols] = ins[r][:, :DH]
            v_ref[:, cols] = ins[r][:, DH:]

    out = jax.ShapeDtypeStruct((rows, kv_heads * DH), jnp.bfloat16)
    return call(body, (out, out), [SMEM] + [VMEM] * kv_heads + [ANY], (VMEM, VMEM))(
        pos, *blocks, after
    )


def per_device(query, key_seq, value_seq, attn_out, grad_out, lse):
    seq_count = lax.axis_size("seq")
    rows = key_seq.shape[0]
    total = rows * seq_count
    kv_heads = key_seq.shape[1] // DH
    heads_here = lse.shape[0]
    copies = seq_count // kv_heads
    pad = -(-heads_here // 8) * 8
    me = lax.axis_index("seq")
    plane, place = me // copies, me % copies
    pos = jnp.stack([plane, place]).astype(jnp.int32)

    def across(x, r):
        turn = [(j, (j + r * copies) % seq_count) for j in range(seq_count)]
        return lax.ppermute(x, "seq", turn)

    def swap(x, s):
        if copies & (copies - 1):
            return inside(x, s)
        return lax.ppermute(x, "seq", [(j, j ^ s) for j in range(seq_count)])

    def inside(x, s):
        turn = [(j, j // copies * copies + (j + s) % copies) for j in range(seq_count)]
        return lax.ppermute(x, "seq", turn)

    def columns(x, n):
        return lax.dynamic_slice_in_dim(x, n % kv_heads * DH, DH, axis=1)

    def pick(x, n):
        return lax.dynamic_index_in_dim(x, n % x.shape[0], 0, keepdims=False)

    got = []
    for r in (0, *range(kv_heads - 1, 0, -1)):
        both = jnp.concatenate([columns(key_seq, plane + r), columns(value_seq, plane + r)], axis=1)
        got.append(across(both, r) if r else both)
    mine = stack(got[:1] + got[:0:-1])
    send = pack(attn_out, grad_out, seq_count, heads_here, pad)
    pieces = [mine] + [swap(mine, s) for s in range(1, copies)]
    grad = lax.all_to_all(send, "seq", split_axis=0, concat_axis=0, tiled=True)
    pieces = [pltpu.with_memory_space_constraint(x, pltpu.HBM) for x in pieces]
    query_local, *parts = attend(pos, query, grad, lse, pieces, min(512, total))
    parts = parts[:1] + [inside(parts[s], s) for s in range(1, copies)]
    back = lax.all_to_all(query_local, "seq", split_axis=0, concat_axis=0, tiled=True)
    query_grad = (
        back.reshape(seq_count, rows, heads_here * DH)
        .transpose(1, 0, 2)
        .reshape(rows, seq_count * heads_here * DH)
    )
    sums = reduce_kv(pos, parts)
    blocks = [sums[0]] + [across(sums[r], r) for r in range(1, kv_heads)]
    key_grad, value_grad = finish_kv(pos, blocks, query_grad)
    return query_grad, key_grad, value_grad


def solution(mesh):
    tokens = P(("dp", "seq"), None)
    return jax.shard_map(
        per_device,
        mesh=mesh,
        in_specs=(P("dp", "seq"), tokens, tokens, tokens, tokens, P("seq", "dp")),
        out_specs=(tokens, tokens, tokens),
        check_vma=False,
    )
```

```python
import jax
import jax.numpy as jnp
from jax import lax
from jax.experimental import pallas as pl
from jax.experimental.pallas import tpu as pltpu
from jax.sharding import PartitionSpec as P

DH = 128
SCALE = DH ** (-0.5)
LOG2E = 1.4426950408889634
NT = (((1,), (1,)), ((), ()))
NN = (((1,), (0,)), ((), ()))
VMEM = pl.BlockSpec(memory_space=pltpu.VMEM)
ANY = pl.BlockSpec(memory_space=pl.ANY)
SMEM = pl.BlockSpec(memory_space=pltpu.SMEM)
LIMIT = 44 << 20


def dot(a, b, dims):
    return lax.dot_general(a, b, dims, preferred_element_type=jnp.float32)


def call(body, out_shape, in_specs, out_specs, flops=0, exps=0, **kw):
    return pl.pallas_call(
        body,
        out_shape=out_shape,
        in_specs=in_specs,
        out_specs=out_specs,
        compiler_params=pltpu.CompilerParams(vmem_limit_bytes=LIMIT),
        cost_estimate=pl.CostEstimate(
            flops=flops, transcendentals=exps, bytes_accessed=4 << 20
        ),
        **kw,
    )


def pack(out, grad, seq_count, heads_here, pad):
    rows = grad.shape[0]
    width = heads_here * DH
    cols = 4 * width if seq_count % 4 == 0 else width
    here = cols // width

    def body(o_ref, g_ref, send_ref):
        at = lax.broadcasted_iota(jnp.int32, (cols, 128), 0) // DH
        at = at // heads_here * pad + at % heads_here
        ones = (at == lax.broadcasted_iota(jnp.int32, (cols, 128), 1)).astype(jnp.bfloat16)
        for n in range(0, seq_count, here):
            c = slice(n * width, n * width + cols)
            prod = g_ref[:, c].astype(jnp.float32) * o_ref[:, c].astype(jnp.float32)
            high = prod.astype(jnp.bfloat16)
            low = (prod - high.astype(jnp.float32)).astype(jnp.bfloat16)
            delta = (dot(high, ones, NN) + dot(low, ones, NN)).T
            if DH > rows:
                fill = jnp.zeros((128, DH - rows), jnp.float32)
                delta = jnp.concatenate([delta, fill], axis=1)
            for d in range(here):
                for h in range(heads_here):
                    c = slice((n + d) * width + h * DH, (n + d) * width + (h + 1) * DH)
                    send_ref[n + d, h * rows : (h + 1) * rows] = g_ref[:, c]
                low = delta[d * pad : (d + 1) * pad].astype(jnp.bfloat16)
                send_ref[n + d, heads_here * rows :] = low

    return call(
        body,
        jax.ShapeDtypeStruct((seq_count, heads_here * rows + pad, DH), jnp.bfloat16),
        [VMEM, VMEM],
        VMEM,
    )(out, grad)


def attend(pos, q, g, lse, pieces, block):
    total, width = q.shape
    heads = width // DH
    copies = len(pieces)
    planes, rows, _ = pieces[0].shape
    owners = block // rows

    def body(pos_ref, q_ref, g_ref, lse_ref, *refs):
        ins, dq_ref, slots = refs[:copies], refs[copies], refs[copies + 1 : 2 * copies + 1]
        kv_ref, l_ref, d_ref, acc_ref, dkv_ref, sems = refs[2 * copies + 1 :]
        plane, place = pos_ref[0], pos_ref[1]
        coming = []
        for s in range(copies):
            source = lax.rem(place - s + copies, copies)
            for r in range(planes):
                owner = lax.rem(plane - r + planes, planes) * copies + source
                start = pl.multiple_of(owner * rows, rows)
                copy = pltpu.make_async_copy(
                    ins[s].at[r], kv_ref.at[pl.ds(start, rows)], sems.at[s, r]
                )
                copy.start()
                coming.append(copy)
        l_ref[...] = lse_ref[...] * LOG2E
        for n in range(total // rows):
            d_ref[:, n * rows : (n + 1) * rows] = g_ref[n, heads * rows :, :rows].astype(jnp.float32)
        for copy in coming:
            copy.wait()
        for k0 in range(0, total, block):
            k1 = k0 + block
            kb, vb = kv_ref[k0:k1, :DH], kv_ref[k0:k1, DH:]
            kt = kb.T
            dk = dv = None
            for q0 in range(k0, total, block):
                q1 = q0 + block
                n0 = q0 // rows
                for h in range(heads):
                    c = slice(h * DH, (h + 1) * DH)
                    qb = q_ref[q0:q1, c]
                    gb = g_ref[n0 : n0 + owners, h * rows : (h + 1) * rows].reshape(block, DH)
                    s = dot(kb, qb, NT) * (SCALE * LOG2E) - l_ref[h : h + 1, q0:q1]
                    if k1 > q0:
                        key_ids = k0 + lax.broadcasted_iota(jnp.int32, s.shape, 0)
                        query_ids = q0 + lax.broadcasted_iota(jnp.int32, s.shape, 1)
                        s = jnp.where(key_ids <= query_ids, s, -1e30)
                    p = jnp.exp2(s)
                    t = dot(p.astype(jnp.bfloat16), gb, NN)
                    dv = t if dv is None else dv + t
                    ds = p * (dot(vb, gb, NT) - d_ref[h : h + 1, q0:q1])
                    ds = ds.astype(jnp.bfloat16)
                    t = dot(ds, qb, NN)
                    dk = t if dk is None else dk + t
                    t = dot(kt, ds, NN)
                    if k0 == 0:
                        acc_ref[c, q0:q1] = t
                    else:
                        acc_ref[c, q0:q1] += t
                    if q0 == k0:
                        done = (acc_ref[c, q0:q1] * SCALE).astype(jnp.bfloat16)
                        dq_ref[q0:q1, c] = done.T
            dkv_ref[k0:k1, :DH] = (dk * SCALE).astype(jnp.bfloat16)
            dkv_ref[k0:k1, DH:] = dv.astype(jnp.bfloat16)
        for s in range(copies):
            target = lax.rem(place + s, copies)
            for r in range(planes):
                start = pl.multiple_of((r * copies + target) * rows, rows)
                slots[s][r] = dkv_ref[pl.ds(start, rows), :]

    part = jax.ShapeDtypeStruct((planes, rows, 2 * DH), jnp.bfloat16)
    return call(
        body,
        (jax.ShapeDtypeStruct((total, width), jnp.bfloat16),) + (part,) * copies,
        [SMEM] + [VMEM] * 3 + [ANY] * copies,
        (VMEM,) * (1 + copies),
        flops=10 * heads * total * total * DH // 2,
        exps=heads * total * total // 2,
        scratch_shapes=[
            pltpu.VMEM((total, 2 * DH), jnp.bfloat16),
            pltpu.VMEM(lse.shape, jnp.float32),
            pltpu.VMEM((g.shape[1] - heads * rows, total), jnp.float32),
            pltpu.VMEM((width, total), jnp.float32),
            pltpu.VMEM((total, 2 * DH), jnp.bfloat16),
            pltpu.SemaphoreType.DMA((copies, planes)),
        ],
    )(pos, q, g, lse, *pieces)


def stack(blocks):
    def body(*refs):
        for n, ref in enumerate(refs[:-1]):
            refs[-1][n] = ref[...]

    out = jax.ShapeDtypeStruct((len(blocks),) + blocks[0].shape, jnp.bfloat16)
    return call(body, out, [VMEM] * len(blocks), VMEM, flops=int(20e9))(*blocks)


def reduce_kv(pos, parts):
    planes, rows, width = parts[0].shape

    def body(pos_ref, *refs):
        ins, outs = refs[: len(parts)], refs[len(parts) :]
        for r in range(planes):
            n = lax.rem(pos_ref[0] + r, planes)
            total = ins[0][n].astype(jnp.float32)
            for part in ins[1:]:
                total = total + part[n].astype(jnp.float32)
            outs[r][...] = total.astype(jnp.bfloat16)

    out = jax.ShapeDtypeStruct((rows, width), jnp.bfloat16)
    return call(
        body,
        (out,) * planes,
        [SMEM] + [VMEM] * len(parts),
        (VMEM,) * planes,
        flops=int(40e9),
    )(pos, *parts)


def finish_kv(pos, blocks, after):
    kv_heads = len(blocks)
    rows = blocks[0].shape[0]

    def body(pos_ref, *refs):
        ins, (_, k_ref, v_ref) = refs[:kv_heads], refs[kv_heads:]
        for r in range(kv_heads):
            g = lax.rem(pos_ref[0] - r + kv_heads, kv_heads)
            cols = pl.ds(pl.multiple_of(g * DH, DH), DH)
            k_ref[:, cols] = ins[r][:, :DH]
            v_ref[:, cols] = ins[r][:, DH:]

    out = jax.ShapeDtypeStruct((rows, kv_heads * DH), jnp.bfloat16)
    return call(body, (out, out), [SMEM] + [VMEM] * kv_heads + [ANY], (VMEM, VMEM))(
        pos, *blocks, after
    )


def per_device(query, key_seq, value_seq, attn_out, grad_out, lse):
    seq_count = lax.axis_size("seq")
    rows = key_seq.shape[0]
    total = rows * seq_count
    kv_heads = key_seq.shape[1] // DH
    heads_here = lse.shape[0]
    copies = seq_count // kv_heads
    pad = -(-heads_here // 8) * 8
    me = lax.axis_index("seq")
    plane, place = me // copies, me % copies
    pos = jnp.stack([plane, place]).astype(jnp.int32)

    def across(x, r):
        turn = [(j, (j + r * copies) % seq_count) for j in range(seq_count)]
        return lax.ppermute(x, "seq", turn)

    def inside(x, s):
        turn = [(j, j // copies * copies + (j + s) % copies) for j in range(seq_count)]
        return lax.ppermute(x, "seq", turn)

    def columns(x, n):
        return lax.dynamic_slice_in_dim(x, n % kv_heads * DH, DH, axis=1)

    def pick(x, n):
        return lax.dynamic_index_in_dim(x, n % x.shape[0], 0, keepdims=False)

    got = []
    for r in range(kv_heads):
        both = jnp.concatenate([columns(key_seq, plane + r), columns(value_seq, plane + r)], axis=1)
        got.append(across(both, r) if r else both)
    mine = stack(got)
    send = pack(attn_out, grad_out, seq_count, heads_here, pad)
    pieces = [mine] + [inside(mine, s) for s in range(1, copies)]
    grad = lax.all_to_all(send, "seq", split_axis=0, concat_axis=0, tiled=True)
    pieces = [pltpu.with_memory_space_constraint(x, pltpu.HBM) for x in pieces]
    query_local, *parts = attend(pos, query, grad, lse, pieces, min(512, total))
    parts = parts[:1] + [inside(parts[s], s) for s in range(1, copies)]
    back = lax.all_to_all(query_local, "seq", split_axis=0, concat_axis=0, tiled=True)
    query_grad = (
        back.reshape(seq_count, rows, heads_here * DH)
        .transpose(1, 0, 2)
        .reshape(rows, seq_count * heads_here * DH)
    )
    sums = reduce_kv(pos, parts)
    blocks = [sums[0]] + [across(sums[r], r) for r in range(1, kv_heads)]
    key_grad, value_grad = finish_kv(pos, blocks, query_grad)
    return query_grad, key_grad, value_grad


def solution(mesh):
    tokens = P(("dp", "seq"), None)
    return jax.shard_map(
        per_device,
        mesh=mesh,
        in_specs=(P("dp", "seq"), tokens, tokens, tokens, tokens, P("seq", "dp")),
        out_specs=(tokens, tokens, tokens),
        check_vma=False,
    )
```
